32 devices in a mesh: groups: 2 (over y), oeig: 4 (over z), ieig: 4 (over x, core).
Axes of the slice: x: 2, y: 2, z: 4, core: 2. Of those that a mesh axis runs over, the one named last changes fastest.
Arguments:
- activations: bfloat16 [1536, 8192], P(('groups', 'ieig'), 'oeig'), parts along dimension 0, may hold values from -6 to 6
- out_grads: bfloat16 [1536, 16384], P(('groups', 'oeig'), 'ieig'), parts along dimension 0, may hold values from -6 to 6
- in_basis: bfloat16 [8192, 8192], P('oeig', 'ieig'), may hold values from -0.0625 to 0.0625
- out_basis: bfloat16 [16384, 16384], P('ieig', 'oeig'), may hold values from -0.046875 to 0.046875
- eigenvalues: bfloat16 [16384, 8192], P('oeig', 'ieig'), may hold values from 0.0099487305 to 10
- query_grads: bfloat16 [2, 16384, 8192], P(None, 'oeig', 'ieig'), may hold values from -6 to 6
- seq_lang: int32 [48], P('groups'), parts along dimension 0, may hold values from 0 to 7, as said below
- query_lang: int32 [2], replicated, may hold values from 0 to 7, as said below
Outputs:
- influence: float32 [1536, 2], P(('groups', 'oeig', 'ieig')), parts along dimension 0
The draws below stay inside these ranges and needn't reach their ends.
There are 2 independent parts, one for each index of `groups`. The reference program is written for one: setup_inputs(seed, part) draws one part's arguments, and reference() takes and returns one part's arrays. A program takes and returns all parts, laid end to end along the dimension named above; an argument that names none is the same for every part. Nothing has to cross between parts.
Inputs may be any that keep to these rules, and one draw needn't show every extreme that they name: `seq_lang`: every language occurs among the sequences of a slab. `query_lang`: the queries have different languages, and one of them has language 8 - 1.
All inputs are finite; a program needn't handle non-finite values.
Results may differ from the reference program's by a relative error of at most 0.018.
Values may be sent and summed in bfloat16 or wider, within the bound.
A program may use at most 320 MiB of HBM per device.

```python
import math
import jax
import jax.numpy as jnp
from jax import lax

OUT = 16384
IN = 8192
TOKENS = 768
SEQ = 32
QUERIES = 2
LANGS = 8
NSEQ = 24


def draw_seq_lang(key, part):
    key = jax.random.fold_in(key, 11)
    first_key, rest_key = jax.random.split(key)
    order = jax.random.permutation(first_key, LANGS).astype(jnp.int32)
    others = jax.random.randint(rest_key, (NSEQ - LANGS,), 0, LANGS, dtype=jnp.int32)
    return jnp.concatenate([order, others]).astype(jnp.int32)


def draw_query_lang(key, part):
    key = jax.random.fold_in(key, 23)
    order_key, place_key = jax.random.split(key)
    order = jax.random.permutation(order_key, LANGS - 1).astype(jnp.int32)
    others = order[:QUERIES]
    place = jax.random.randint(place_key, (), 0, QUERIES, dtype=jnp.int32)
    position = jnp.arange(QUERIES, dtype=jnp.int32)
    before = others[position]
    after = others[jnp.maximum(position - 1, 0)]
    picked = jnp.where(position < place, before, after)
    return jnp.where(position == place, LANGS - 1, picked).astype(jnp.int32)


def steps_of(own_key, shape, shards, smallest, top_value):
    gain, own = 1.0, jax.random.fold_in(own_key, 6)
    for dim, shards_of in shards:
        steps = jnp.exp(jax.random.uniform(jax.random.fold_in(own, dim), (shards_of,), jnp.float32, smallest / len(shards), top_value / len(shards)))
        gain = gain * jnp.repeat(steps, shape[dim] // shards_of).reshape([-1 if axis == dim else 1 for axis in range(len(shape))])
    return gain


def noise(rng, dims, spread, bound, cuts=(), kind=jnp.bfloat16):
    result = spread * jax.random.normal(rng, dims, jnp.float32)
    if cuts:
        result = result * steps_of(rng, dims, cuts, -0.22, 0.18)
    return jnp.clip(result, -bound, bound).astype(kind)


def setup_inputs(seed: int = 0, part: int = 0) -> dict:
    splits = jax.random.split(jax.random.key(seed), 9)
    part_keys = jax.random.split(jax.random.fold_in(splits[8], part), 9)
    activations = noise(part_keys[0], (TOKENS, IN), 1.0, 6.0, ((0, 4), (1, 4)))
    out_grads = noise(part_keys[1], (TOKENS, OUT), 1.0, 6.0, ((0, 4), (1, 4)))
    in_basis = noise(splits[2], (IN, IN), IN ** -0.5, 0.0625, ((0, 4), (1, 4)))
    out_basis = noise(splits[3], (OUT, OUT), OUT ** -0.5, 0.046875, ((0, 4), (1, 4)))
    eigenvalues = jnp.clip(jnp.exp(math.log(10.0) - 6.912895 * jax.random.uniform(splits[4], (OUT, IN), jnp.float32) ** steps_of(splits[4], (OUT, IN), ((0, 4), (1, 4)), -0.2, 0.2)), 0.0099487305, 10.0).astype(jnp.bfloat16)
    query_grads = noise(splits[5], (QUERIES, OUT, IN), 1.0, 6.0, ((1, 4), (2, 4)))
    seq_lang = draw_seq_lang(jax.random.fold_in(jax.random.fold_in(splits[8], part), 71), part)
    query_lang = draw_query_lang(jax.random.fold_in(splits[8], 71), part)
    return {"activations": activations, "out_grads": out_grads, "in_basis": in_basis, "out_basis": out_basis, "eigenvalues": eigenvalues, "query_grads": query_grads, "seq_lang": seq_lang, "query_lang": query_lang}


DAMPING = 0.1

def reference(activations, out_grads, in_basis, out_basis, eigenvalues, query_grads, seq_lang, query_lang):
    rotated_in = jnp.dot(activations, in_basis, preferred_element_type=jnp.float32).astype(jnp.bfloat16)
    rotated_out = jnp.dot(out_grads, out_basis, preferred_element_type=jnp.float32).astype(jnp.bfloat16)
    eigen_plus = eigenvalues.astype(jnp.float32) + DAMPING
    rotated_wide = rotated_out.astype(jnp.float32)

    def one_query(query_block):
        damped = (query_block.astype(jnp.float32) / eigen_plus).astype(jnp.bfloat16)
        contracted = jnp.dot(rotated_in, damped.T, preferred_element_type=jnp.float32)
        return lax.optimization_barrier(jnp.sum(rotated_wide * contracted, axis=1))
    score = lax.map(one_query, query_grads).T
    seq_index = jnp.arange(TOKENS, dtype=jnp.int32) // SEQ
    row_lang = seq_lang[seq_index]
    matched = row_lang[:, None] == query_lang[None, :]
    factor = jnp.where(matched, 1.0, 0.5).astype(jnp.float32)
    return score * (1.0 / math.sqrt(OUT * IN)) * factor
```

```python
import functools
import math

import jax
import jax.numpy as jnp
from jax import lax
from jax.experimental import pallas as pl
from jax.experimental.pallas import tpu as pltpu
from jax.sharding import PartitionSpec as P

OUT = 16384
IN = 8192
SEQ = 32


DAMPING = 0.1
MESH = pl.DeviceIdType.MESH
F32 = jnp.float32
BF16 = jnp.bfloat16

SIDE = 4
PIECES = 2
TILE = 512
DROWS = 128
STRIP = 16


def kernel(
    act_hbm, og_hbm, ib_hbm, ob_hbm, eig_hbm, qg_hbm,
    out_ref, d_hbm,
    og, act, rip, prec, srec, ro, crecv, xrecv, frecv, w, wbuf, qbuf, ebuf, dbuf, sc, rsc,
    lsem, wsem, qsem, esem, dsem,
    ring_s, ring_r, act_s, act_r, c_s, c_r, x_s, x_r, f_s, f_r, p_s, p_r, s_s, s_r, sc_s, sc_r,
):
    a, b = lax.axis_index("oeig"), lax.axis_index("ieig")
    me = a * SIDE + b
    rows = og.shape[1]
    piece = rows // PIECES
    chunks = SIDE * PIECES
    width = og.shape[2]
    half = width // 2
    span = act.shape[2]
    queries = d_hbm.shape[0]
    core = lax.rem(b, 2)
    mate = b + 1 - 2 * core
    across = lax.rem(b + 2, SIDE)
    ring_next = lax.rem(2 * a + 1, 5)

    def ring_prev(i):
        return lax.rem(3 * i + 2, 5)

    owner = [a]
    for _ in range(SIDE - 1):
        owner.append(ring_prev(owner[-1]))
    act_owner = [b, mate, across, lax.rem(mate + 2, SIDE)]

    def remote(src, dst, send, recv, to_a, to_b):
        return pltpu.make_async_remote_copy(
            src_ref=src, dst_ref=dst, send_sem=send, recv_sem=recv,
            device_id={"oeig": to_a, "ieig": to_b}, device_id_type=MESH,
        )

    barrier = pltpu.get_barrier_semaphore()
    others = SIDE * SIDE - 1

    @pl.loop(1, others + 1)
    def _(k):
        peer = lax.rem(me + k, SIDE * SIDE)
        pl.semaphore_signal(
            barrier, inc=1, device_id={"oeig": peer // SIDE, "ieig": lax.rem(peer, SIDE)},
            device_id_type=MESH,
        )

    own_og = pltpu.make_async_copy(og_hbm, og.at[0], lsem.at[0])
    own_act = pltpu.make_async_copy(act_hbm, act.at[0], lsem.at[1])
    own_og.start()
    own_act.start()
    pl.semaphore_wait(barrier, others)

    def ring(step):
        src = og_hbm if step == 1 else og.at[step - 1]
        return remote(src, og.at[step], ring_s.at[step], ring_r.at[step], ring_next, b)

    act_x = remote(act_hbm, act.at[2], act_s.at[2], act_r.at[2], a, across)
    act_c = remote(act_hbm, act.at[1], act_s.at[1], act_r.at[1], a, mate)
    act_f = remote(act.at[2], act.at[3], act_s.at[3], act_r.at[3], a, mate)
    act_x.start()
    act_c.start()
    ring(1).start()

    def stream(count, source, view, compute):
        def copy(k):
            slot = lax.rem(k, 2)
            return pltpu.make_async_copy(source(k), view(slot), wsem.at[slot])

        copy(jnp.int32(0)).start()

        @pl.loop(0, count)
        def _(k):
            @pl.when(k + 1 < count)
            def _():
                copy(k + 1).start()

            copy(k).wait()
            compute(k, view(lax.rem(k, 2)))

    def columns(k):
        return pl.ds(pl.multiple_of(k * TILE, TILE), TILE)

    def strips(count, body):
        @pl.loop(0, count // STRIP)
        def _(i):
            body(pl.ds(pl.multiple_of(i * STRIP, STRIP), STRIP))

    my_half = pl.ds(pl.multiple_of(core * half, half), half)
    other_half = pl.ds(pl.multiple_of((1 - core) * half, half), half)
    my_rows, other_rows = my_half, other_half

    def to_mate(s):
        return remote(ro.at[s, :, other_half], crecv.at[s], c_s.at[s], c_r.at[s], a, mate)

    def to_across(s):
        return remote(crecv.at[s], xrecv.at[s], x_s.at[s], x_r.at[s], a, across)

    def whole_to_mate(s):
        return remote(ro.at[s, :, my_half], frecv.at[s], f_s.at[s], f_r.at[s], a, mate)

    def rotate_out(s):
        def compute(k, tile):
            part = jnp.dot(og[s], tile[...], preferred_element_type=F32)
            ro[s, :, columns(k)] = part.astype(BF16)

        stream(width // TILE, lambda k: ob_hbm.at[:, columns(k)], lambda v: wbuf.at[v], compute)
        to_mate(s).start()

    def sum_cores(s):
        to_mate(s).wait_recv()

        def body(r):
            crecv[s, r, :] = (
                crecv[s, r, :].astype(F32) + ro[s, r, my_half].astype(F32)
            ).astype(BF16)

        strips(rows, body)
        to_across(s).start()

    def sum_across(s):
        to_across(s).wait_recv()

        def body(r):
            ro[s, r, my_half] = (
                crecv[s, r, :].astype(F32) + xrecv[s, r, :].astype(F32)
            ).astype(BF16)

        strips(rows, body)
        whole_to_mate(s).start()

    def rotate_in():
        def compute(k, tile):
            for s in range(SIDE):
                part = jnp.dot(act[s], tile[...], preferred_element_type=F32).astype(BF16)
                for h in range(PIECES):
                    rip[act_owner[s] * PIECES + h, :, columns(k)] = part[
                        h * piece : (h + 1) * piece
                    ]

        stream(
            span // TILE, lambda k: ib_hbm.at[:, columns(k)],
            lambda v: wbuf.at[v, pl.ds(0, span), :], compute,
        )

    def damp(first, last):
        def block(k):
            return pl.ds(pl.multiple_of(k * DROWS, DROWS), DROWS)

        def loads(k):
            v = lax.rem(k, 2)
            return (
                pltpu.make_async_copy(qg_hbm.at[:, block(k), :], qbuf.at[v], qsem.at[v]),
                pltpu.make_async_copy(eig_hbm.at[block(k), :], ebuf.at[v], esem.at[v]),
            )

        def store(k):
            v = lax.rem(k, 2)
            return pltpu.make_async_copy(dbuf.at[v], d_hbm.at[:, block(k), :], dsem.at[v])

        for c in loads(jnp.int32(first)):
            c.start()

        @pl.loop(first, last)
        def _(k):
            v = lax.rem(k, 2)

            @pl.when(k + 1 < last)
            def _():
                for c in loads(k + 1):
                    c.start()

            for c in loads(k):
                c.wait()

            @pl.when(k >= first + 2)
            def _():
                store(k - 2).wait()

            def body(r):
                inv = 1.0 / (ebuf[v, r, :].astype(F32) + DAMPING)
                for m in range(queries):
                    dbuf[v, m, r, :] = (qbuf[v, m, r, :].astype(F32) * inv).astype(BF16)

            strips(DROWS, body)
            store(k).start()

        for k in (last - 2, last - 1):
            store(jnp.int32(k)).wait()

    tiles = span // TILE

    def contract(s):
        whole_to_mate(s).wait_recv()

        def compute(k, tile):
            mine = jnp.dot(ro[s, :, my_half], tile[my_rows, :], preferred_element_type=F32)
            w[s, :, columns(k)] = mine + jnp.dot(
                frecv[s], tile[other_rows, :], preferred_element_type=F32
            )

        stream(
            queries * tiles,
            lambda k: d_hbm.at[k // tiles, :, columns(lax.rem(k, tiles))],
            lambda v: wbuf.at[v], compute,
        )

    last_a = SIDE - 1
    up = lax.rem(a + 1, SIDE)
    down = lax.rem(a + last_a, SIDE)

    def going_up(c):
        return remote(prec.at[c], prec.at[c], p_s.at[c], p_r.at[c], up, b)

    def outgoing(c):
        start = pl.multiple_of(lax.rem(c, PIECES) * piece, piece)
        return act.at[lax.div(c, PIECES), pl.ds(start, piece), :]

    def going_down(c):
        return remote(outgoing(c), srec.at[c], s_s.at[c], s_r.at[c], down, b)

    def chain(step):
        c = step - a

        @pl.when((c >= 0) & (c < chunks))
        def _():
            @pl.when(a == 0)
            def _():
                def body(r):
                    prec[c, r, :] = rip[c, r, :]

                strips(piece, body)

            @pl.when(a > 0)
            def _():
                going_up(c).wait_recv()

                def body(r):
                    prec[c, r, :] = (
                        prec[c, r, :].astype(F32) + rip[c, r, :].astype(F32)
                    ).astype(BF16)

                strips(piece, body)

            @pl.when(a < last_a)
            def _():
                going_up(c).start()

        e = step - (last_a - a)

        @pl.when((e >= 0) & (e < chunks))
        def _():
            @pl.when(a == last_a)
            def _():
                def body(r):
                    srec[e, r, :] = jnp.zeros_like(srec[e, r, :])
                    outgoing(e)[r, :] = rip[e, r, :]

                strips(piece, body)

            @pl.when(a < last_a)
            def _():
                going_down(e).wait_recv()

                def body(r):
                    outgoing(e)[r, :] = (
                        srec[e, r, :].astype(F32) + rip[e, r, :].astype(F32)
                    ).astype(BF16)

                strips(piece, body)

            @pl.when(a > 0)
            def _():
                going_down(e).start()

    dtiles = d_hbm.shape[1] // DROWS

    own_og.wait()
    rotate_out(0)
    own_act.wait()
    act_x.wait_recv()
    act_f.start()
    act_c.wait_recv()
    sum_cores(0)
    act_f.wait_recv()
    rotate_in()
    for c in (act_x, act_c, act_f):
        c.wait_send()
    damp(0, dtiles // 2)
    sum_across(0)

    ring(1).wait_recv()
    ring(2).start()
    rotate_out(1)
    damp(dtiles // 2, dtiles)
    sum_cores(1)

    ring(2).wait_recv()
    ring(3).start()
    chain(0)
    rotate_out(2)
    sum_across(1)
    chain(1)
    contract(0)
    sum_cores(2)
    chain(2)
    contract(1)
    sum_across(2)
    chain(3)

    ring(3).wait_recv()
    rotate_out(3)
    chain(4)
    sum_cores(3)
    chain(5)
    contract(2)
    sum_across(3)
    chain(6)
    contract(3)
    for step in range(7, chunks + last_a):
        chain(step)

    lane = lax.broadcasted_iota(jnp.int32, (STRIP, sc.shape[2]), 1)
    per = sc.shape[1]
    for s in range(SIDE):
        for h in range(PIECES):
            c = owner[s] * PIECES + h

            @pl.loop(0, piece // STRIP)
            def _(i):
                r = pl.ds(pl.multiple_of(i * STRIP, STRIP), STRIP)
                total = prec[c, r, :].astype(F32) + srec[c, r, :].astype(F32)
                wr = pl.ds(pl.multiple_of(h * piece + i * STRIP, STRIP), STRIP)
                packed = jnp.zeros(lane.shape, F32)
                for m in range(queries):
                    got = jnp.sum(
                        total * w[s, wr, m * span : (m + 1) * span], axis=1, keepdims=True
                    )
                    packed = jnp.where(lane == m, got, packed)
                row = owner[s] * rows + h * piece + i * STRIP
                sc[row // per, pl.ds(pl.multiple_of(lax.rem(row, per), STRIP), STRIP), :] = packed

    def score(k):
        peer = lax.rem(me + k, SIDE * SIDE)
        return remote(
            sc.at[peer], rsc.at[k], sc_s.at[k], sc_r.at[k], peer // SIDE, lax.rem(peer, SIDE)
        )

    @pl.loop(1, others + 1)
    def _(k):
        score(k).start()

    rsc[0] = sc[me]

    for step in range(1, SIDE):
        ring(step).wait_send()
    for s in range(SIDE):
        to_mate(s).wait_send()
        to_across(s).wait_send()
        whole_to_mate(s).wait_send()

    @pl.loop(0, chunks)
    def _(c):
        @pl.when(a < last_a)
        def _():
            going_up(c).wait_send()

        @pl.when(a > 0)
        def _():
            going_down(c).wait_send()

    @pl.loop(1, others + 1)
    def _(k):
        score(k).wait()

    total = rsc[0]
    for k in range(1, SIDE * SIDE):
        total = total + rsc[k]
    out_ref[...] = total


def fused_scores(activations, out_grads, in_basis, out_basis, eigenvalues, query_grads):
    rows, span = activations.shape
    width = out_grads.shape[1]
    queries = query_grads.shape[0]
    chunks, piece = SIDE * PIECES, rows // PIECES
    devices = SIDE * SIDE
    per = SIDE * rows // devices
    vmem = pltpu.VMEM
    dma = pltpu.SemaphoreType.DMA
    any_space = pl.BlockSpec(memory_space=pl.ANY)
    out, _ = pl.pallas_call(
        kernel,
        out_shape=(
            jax.ShapeDtypeStruct((per, 128), F32),
            jax.ShapeDtypeStruct(query_grads.shape, BF16),
        ),
        in_specs=[any_space] * 6,
        out_specs=(pl.BlockSpec(memory_space=pltpu.VMEM), any_space),
        scratch_shapes=[
            vmem((SIDE, rows, width), BF16),
            vmem((SIDE, rows, span), BF16),
            vmem((chunks, piece, span), BF16),
            vmem((chunks, piece, span), BF16),
            vmem((chunks, piece, span), BF16),
            vmem((SIDE, rows, width), BF16),
            vmem((SIDE, rows, width // 2), BF16),
            vmem((SIDE, rows, width // 2), BF16),
            vmem((SIDE, rows, width // 2), BF16),
            vmem((SIDE, rows, queries * span), F32),
            vmem((2, width, TILE), BF16),
            vmem((2, queries, DROWS, span), BF16),
            vmem((2, DROWS, span), BF16),
            vmem((2, queries, DROWS, span), BF16),
            vmem((devices, per, 128), F32),
            vmem((devices, per, 128), F32),
        ]
        + [dma((2,))] * 5
        + [dma((SIDE,))] * 10
        + [dma((chunks,))] * 4
        + [dma((devices,))] * 2,
        compiler_params=pltpu.CompilerParams(
            collective_id=0, has_side_effects=True, vmem_limit_bytes=63 * 1024 * 1024
        ),
        cost_estimate=pl.CostEstimate(
            flops=2 * SIDE * rows * (width * width + span * span + queries * width * span),
            bytes_accessed=2 * (8 * width * width + span * span), transcendentals=0,
        ),
    )(activations, out_grads, in_basis, out_basis, eigenvalues, query_grads)
    return out[:, :queries]


def plain_scores(activations, out_grads, in_basis, out_basis, eigenvalues, query_grads):
    partial_out = jnp.dot(
        lax.all_gather(out_grads, "oeig", axis=0, tiled=True),
        out_basis,
        preferred_element_type=jnp.float32,
    )
    rotated_out = lax.psum(partial_out.astype(jnp.bfloat16), "ieig")
    partial_in = jnp.dot(
        lax.all_gather(activations, "ieig", axis=0, tiled=True),
        in_basis,
        preferred_element_type=jnp.float32,
    )
    rotated_in = lax.psum(partial_in.astype(jnp.bfloat16), "oeig")
    damped = (query_grads.astype(jnp.float32) / (eigenvalues.astype(jnp.float32) + DAMPING)).astype(
        jnp.bfloat16
    )
    contracted = jnp.einsum("ti,moi->mto", rotated_in, damped, preferred_element_type=jnp.float32)
    partial_score = jnp.sum(contracted * rotated_out.astype(jnp.float32)[None], axis=2).T
    row_count = partial_score.shape[0] // lax.axis_size(("oeig", "ieig"))
    first_row = lax.axis_index(("oeig", "ieig")) * row_count
    summed = lax.psum(partial_score, ("oeig", "ieig"))
    return lax.dynamic_slice_in_dim(summed, first_row, row_count, 0)


def local(
    fused, activations, out_grads, in_basis, out_basis, eigenvalues, query_grads, seq_lang,
    query_lang,
):
    scores = fused_scores if fused else plain_scores
    own_rows = scores(activations, out_grads, in_basis, out_basis, eigenvalues, query_grads)
    row_count = own_rows.shape[0]
    first_row = lax.axis_index(("oeig", "ieig")) * row_count
    seq_index = (first_row + jnp.arange(row_count, dtype=jnp.int32)) // SEQ
    onehot = seq_index[:, None] == jnp.arange(seq_lang.shape[0], dtype=jnp.int32)[None, :]
    row_lang = jnp.sum(jnp.where(onehot, seq_lang[None, :], 0), axis=1)
    matched = row_lang[:, None] == query_lang[None, :]
    factor = jnp.where(matched, 1.0, 0.5).astype(jnp.float32)
    return own_rows * (1.0 / math.sqrt(OUT * IN)) * factor


def solution(mesh):
    fused = mesh.shape["oeig"] == SIDE and mesh.shape["ieig"] == SIDE
    return jax.shard_map(
        functools.partial(local, fused),
        mesh=mesh,
        in_specs=(
            P(("groups", "ieig"), "oeig"),
            P(("groups", "oeig"), "ieig"),
            P("oeig", "ieig"),
            P("ieig", "oeig"),
            P("oeig", "ieig"),
            P(None, "oeig", "ieig"),
            P("groups"),
            P(),
        ),
        out_specs=P(("groups", "oeig", "ieig"), None),
        check_vma=False,
    )
```

```python
import functools
import math

import jax
import jax.numpy as jnp
from jax import lax
from jax.experimental import pallas as pl
from jax.experimental.pallas import tpu as pltpu
from jax.sharding import PartitionSpec as P

OUT = 16384
IN = 8192
SEQ = 32


DAMPING = 0.1
MESH = pl.DeviceIdType.MESH
F32 = jnp.float32
BF16 = jnp.bfloat16

SIDE = 4
PIECES = 2
TILE = 512
DROWS = 128
STRIP = 16


def reciprocal(x):
    guess = pl.reciprocal(x, approx=True)
    return guess * (2.0 - x * guess)


def kernel(
    act_hbm, og_hbm, ib_hbm, ob_hbm, eig_hbm, qg_hbm,
    out_ref, d_hbm,
    og, act, rip, prec, srec, ro, crecv, xrecv, frecv, w, wbuf, qbuf, ebuf, dbuf, sc, rsc,
    lsem, wsem, qsem, esem, dsem,
    ring_s, ring_r, act_s, act_r, c_s, c_r, x_s, x_r, f_s, f_r, p_s, p_r, s_s, s_r, sc_s, sc_r,
):
    a, b = lax.axis_index("oeig"), lax.axis_index("ieig")
    me = a * SIDE + b
    rows = og.shape[1]
    piece = rows // PIECES
    chunks = SIDE * PIECES
    width = og.shape[2]
    half = width // 2
    span = act.shape[2]
    queries = d_hbm.shape[0]
    core = lax.rem(b, 2)
    mate = b + 1 - 2 * core
    across = lax.rem(b + 2, SIDE)
    ring_next = lax.rem(2 * a + 1, 5)
    act_owner = [b, mate, across, lax.rem(mate + 2, SIDE)]

    def remote(src, dst, send, recv, to_a, to_b):
        return pltpu.make_async_remote_copy(
            src_ref=src, dst_ref=dst, send_sem=send, recv_sem=recv,
            device_id={"oeig": to_a, "ieig": to_b}, device_id_type=MESH,
        )

    barrier = pltpu.get_barrier_semaphore()
    others = SIDE * SIDE - 1

    @pl.loop(1, others + 1)
    def _(k):
        peer = lax.rem(me + k, SIDE * SIDE)
        pl.semaphore_signal(
            barrier, inc=1, device_id={"oeig": peer // SIDE, "ieig": lax.rem(peer, SIDE)},
            device_id_type=MESH,
        )

    own_og = pltpu.make_async_copy(og_hbm, og.at[0], lsem.at[0])
    own_act = pltpu.make_async_copy(act_hbm, act.at[0], lsem.at[1])
    own_og.start()
    own_act.start()
    pl.semaphore_wait(barrier, others)

    def ring(step):
        src = og_hbm if step == 1 else og.at[step - 1]
        return remote(src, og.at[step], ring_s.at[step], ring_r.at[step], ring_next, b)

    act_x = remote(act_hbm, act.at[2], act_s.at[2], act_r.at[2], a, across)
    act_c = remote(act_hbm, act.at[1], act_s.at[1], act_r.at[1], a, mate)
    act_f = remote(act.at[2], act.at[3], act_s.at[3], act_r.at[3], a, mate)
    act_x.start()
    act_c.start()
    ring(1).start()

    def stream(count, source, view, compute):
        def copy(k):
            slot = lax.rem(k, 2)
            return pltpu.make_async_copy(source(k), view(slot), wsem.at[slot])

        copy(jnp.int32(0)).start()

        @pl.loop(0, count)
        def _(k):
            @pl.when(k + 1 < count)
            def _():
                copy(k + 1).start()

            copy(k).wait()
            compute(k, view(lax.rem(k, 2)))

    def columns(k):
        return pl.ds(pl.multiple_of(k * TILE, TILE), TILE)

    def strips(count, body):
        @pl.loop(0, count // STRIP)
        def _(i):
            body(pl.ds(pl.multiple_of(i * STRIP, STRIP), STRIP))

    my_half = pl.ds(pl.multiple_of(core * half, half), half)
    other_half = pl.ds(pl.multiple_of((1 - core) * half, half), half)
    my_rows, other_rows = my_half, other_half

    def to_mate(s):
        return remote(ro.at[s, :, other_half], crecv.at[s], c_s.at[s], c_r.at[s], a, mate)

    def to_across(s):
        return remote(crecv.at[s], xrecv.at[s], x_s.at[s], x_r.at[s], a, across)

    def whole_to_mate(s):
        return remote(ro.at[s, :, my_half], frecv.at[s], f_s.at[s], f_r.at[s], a, mate)

    def rotate_out(s):
        def compute(k, tile):
            part = jnp.dot(og[s], tile[...], preferred_element_type=F32)
            ro[s, :, columns(k)] = part.astype(BF16)

        stream(width // TILE, lambda k: ob_hbm.at[:, columns(k)], lambda v: wbuf.at[v], compute)
        to_mate(s).start()

    def sum_cores(s):
        to_mate(s).wait_recv()

        def body(r):
            crecv[s, r, :] = (
                crecv[s, r, :].astype(F32) + ro[s, r, my_half].astype(F32)
            ).astype(BF16)

        strips(rows, body)
        to_across(s).start()

    def sum_across(s):
        to_across(s).wait_recv()

        def body(r):
            ro[s, r, my_half] = (
                crecv[s, r, :].astype(F32) + xrecv[s, r, :].astype(F32)
            ).astype(BF16)

        strips(rows, body)
        whole_to_mate(s).start()

    def rotate_in():
        def compute(k, tile):
            for s in range(SIDE):
                part = jnp.dot(act[s], tile[...], preferred_element_type=F32).astype(BF16)
                for h in range(PIECES):
                    rip[act_owner[s] * PIECES + h, :, columns(k)] = part[
                        h * piece : (h + 1) * piece
                    ]

        stream(
            span // TILE, lambda k: ib_hbm.at[:, columns(k)],
            lambda v: wbuf.at[v, pl.ds(0, span), :], compute,
        )

    def damp(first, last):
        def block(k):
            return pl.ds(pl.multiple_of(k * DROWS, DROWS), DROWS)

        def loads(k):
            v = lax.rem(k, 2)
            return (
                pltpu.make_async_copy(qg_hbm.at[:, block(k), :], qbuf.at[v], qsem.at[v]),
                pltpu.make_async_copy(eig_hbm.at[block(k), :], ebuf.at[v], esem.at[v]),
            )

        def store(k):
            v = lax.rem(k, 2)
            return pltpu.make_async_copy(dbuf.at[v], d_hbm.at[:, block(k), :], dsem.at[v])

        for c in loads(jnp.int32(first)):
            c.start()

        @pl.loop(first, last)
        def _(k):
            v = lax.rem(k, 2)

            @pl.when(k + 1 < last)
            def _():
                for c in loads(k + 1):
                    c.start()

            for c in loads(k):
                c.wait()

            @pl.when(k >= first + 2)
            def _():
                store(k - 2).wait()

            def body(r):
                inv = reciprocal(ebuf[v, r, :].astype(F32) + DAMPING)
                for m in range(queries):
                    dbuf[v, m, r, :] = (qbuf[v, m, r, :].astype(F32) * inv).astype(BF16)

            strips(DROWS, body)
            store(k).start()

        for k in (last - 2, last - 1):
            store(jnp.int32(k)).wait()

    tiles = span // TILE

    def contract(s, count):
        for k in range(s, s + count):
            whole_to_mate(k).wait_recv()
        slots = pl.ds(s, count)

        def compute(k, tile):
            mine = ro[slots, :, my_half].reshape(count * rows, half)
            theirs = frecv[slots].reshape(count * rows, half)
            got = jnp.dot(mine, tile[my_rows, :], preferred_element_type=F32)
            got = got + jnp.dot(theirs, tile[other_rows, :], preferred_element_type=F32)
            w[slots, :, columns(k)] = got.reshape(count, rows, TILE)

        stream(
            queries * tiles,
            lambda k: d_hbm.at[k // tiles, :, columns(lax.rem(k, tiles))],
            lambda v: wbuf.at[v], compute,
        )

    last_a = SIDE - 1
    up = lax.rem(a + 1, SIDE)
    down = lax.rem(a + last_a, SIDE)

    def going_up(c):
        return remote(prec.at[c], prec.at[c], p_s.at[c], p_r.at[c], up, b)

    def outgoing(c):
        start = pl.multiple_of(lax.rem(c, PIECES) * piece, piece)
        return act.at[lax.div(c, PIECES), pl.ds(start, piece), :]

    def going_down(c):
        return remote(outgoing(c), srec.at[c], s_s.at[c], s_r.at[c], down, b)

    def chain(step):
        c = step - a

        @pl.when((c >= 0) & (c < chunks))
        def _():
            @pl.when(a == 0)
            def _():
                def body(r):
                    prec[c, r, :] = rip[c, r, :]

                strips(piece, body)

            @pl.when(a > 0)
            def _():
                going_up(c).wait_recv()

                def body(r):
                    prec[c, r, :] = (
                        prec[c, r, :].astype(F32) + rip[c, r, :].astype(F32)
                    ).astype(BF16)

                strips(piece, body)

            @pl.when(a < last_a)
            def _():
                going_up(c).start()

        e = step - (last_a - a)

        @pl.when((e >= 0) & (e < chunks))
        def _():
            @pl.when(a == last_a)
            def _():
                def body(r):
                    srec[e, r, :] = jnp.zeros_like(srec[e, r, :])
                    outgoing(e)[r, :] = rip[e, r, :]

                strips(piece, body)

            @pl.when(a < last_a)
            def _():
                going_down(e).wait_recv()

                def body(r):
                    outgoing(e)[r, :] = (
                        srec[e, r, :].astype(F32) + rip[e, r, :].astype(F32)
                    ).astype(BF16)

                strips(piece, body)

            @pl.when(a > 0)
            def _():
                going_down(e).start()

    lane = lax.broadcasted_iota(jnp.int32, (STRIP, sc.shape[2]), 1)
    per = sc.shape[1]
    parcels = piece // per

    def place(i):
        return i + (i // 2) * (1 - 2 * lax.rem(i, 2))

    def score(peer):
        k = lax.rem(peer - me + SIDE * SIDE, SIDE * SIDE)
        return k, remote(
            sc.at[peer], rsc.at[k], sc_s.at[k], sc_r.at[k], peer // SIDE, peer % SIDE
        )

    def finish(c):
        j, h = c // PIECES, c % PIECES
        s = lax.rem(place(a) - (j ^ (j >> 1)) + SIDE, SIDE)

        @pl.loop(0, piece // STRIP)
        def _(i):
            r = pl.ds(pl.multiple_of(i * STRIP, STRIP), STRIP)
            total = prec[c, r, :].astype(F32) + srec[c, r, :].astype(F32)
            wr = pl.ds(pl.multiple_of(h * piece + i * STRIP, STRIP), STRIP)
            packed = jnp.zeros(lane.shape, F32)
            for m in range(queries):
                got = jnp.sum(
                    total * w[s, wr, m * span : (m + 1) * span], axis=1, keepdims=True
                )
                packed = jnp.where(lane == m, got, packed)
            row = i * STRIP
            at = pl.ds(pl.multiple_of(lax.rem(row, per), STRIP), STRIP)
            sc[c * parcels + lax.div(row, per), at, :] = packed

        for peer in range(c * parcels, (c + 1) * parcels):
            k, copy = score(peer)

            @pl.when(k == 0)
            def _():
                rsc[0] = sc[peer]

            @pl.when(k > 0)
            def _():
                copy.start()

    dtiles = d_hbm.shape[1] // DROWS

    own_og.wait()
    rotate_out(0)
    own_act.wait()
    act_x.wait_recv()
    act_f.start()
    act_c.wait_recv()
    sum_cores(0)
    act_f.wait_recv()
    rotate_in()
    for c in (act_x, act_c, act_f):
        c.wait_send()
    chain(0)
    damp(0, dtiles // 2)
    sum_across(0)

    ring(1).wait_recv()
    ring(2).start()
    rotate_out(1)
    chain(1)
    damp(dtiles // 2, dtiles)
    sum_cores(1)
    chain(2)

    ring(2).wait_recv()
    ring(3).start()
    rotate_out(2)
    sum_across(1)
    chain(3)
    contract(0, 2)
    sum_cores(2)
    chain(4)
    sum_across(2)
    chain(5)

    ring(3).wait_recv()
    rotate_out(3)
    chain(6)
    sum_cores(3)
    contract(2, 1)
    chain(7)
    sum_across(3)
    chain(8)
    contract(3, 1)
    done = 0
    for step in range(8, chunks + last_a):
        if step > 8:
            chain(step)
        while done <= step - last_a:
            finish(done)
            done += 1

    for step in range(1, SIDE):
        ring(step).wait_send()
    for s in range(SIDE):
        to_mate(s).wait_send()
        to_across(s).wait_send()
        whole_to_mate(s).wait_send()

    @pl.loop(0, chunks)
    def _(c):
        @pl.when(a < last_a)
        def _():
            going_up(c).wait_send()

        @pl.when(a > 0)
        def _():
            going_down(c).wait_send()

    for peer in range(SIDE * SIDE):
        k, copy = score(peer)

        @pl.when(k > 0)
        def _():
            copy.wait()

    total = rsc[0]
    for k in range(1, SIDE * SIDE):
        total = total + rsc[k]
    out_ref[...] = total


def fused_scores(activations, out_grads, in_basis, out_basis, eigenvalues, query_grads):
    rows, span = activations.shape
    width = out_grads.shape[1]
    queries = query_grads.shape[0]
    chunks, piece = SIDE * PIECES, rows // PIECES
    devices = SIDE * SIDE
    per = SIDE * rows // devices
    vmem = pltpu.VMEM
    dma = pltpu.SemaphoreType.DMA
    any_space = pl.BlockSpec(memory_space=pl.ANY)
    out, _ = pl.pallas_call(
        kernel,
        out_shape=(
            jax.ShapeDtypeStruct((per, 128), F32),
            jax.ShapeDtypeStruct(query_grads.shape, BF16),
        ),
        in_specs=[any_space] * 6,
        out_specs=(pl.BlockSpec(memory_space=pltpu.VMEM), any_space),
        scratch_shapes=[
            vmem((SIDE, rows, width), BF16),
            vmem((SIDE, rows, span), BF16),
            vmem((chunks, piece, span), BF16),
            vmem((chunks, piece, span), BF16),
            vmem((chunks, piece, span), BF16),
            vmem((SIDE, rows, width), BF16),
            vmem((SIDE, rows, width // 2), BF16),
            vmem((SIDE, rows, width // 2), BF16),
            vmem((SIDE, rows, width // 2), BF16),
            vmem((SIDE, rows, queries * span), F32),
            vmem((2, width, TILE), BF16),
            vmem((2, queries, DROWS, span), BF16),
            vmem((2, DROWS, span), BF16),
            vmem((2, queries, DROWS, span), BF16),
            vmem((devices, per, 128), F32),
            vmem((devices, per, 128), F32),
        ]
        + [dma((2,))] * 5
        + [dma((SIDE,))] * 10
        + [dma((chunks,))] * 4
        + [dma((devices,))] * 2,
        compiler_params=pltpu.CompilerParams(
            collective_id=0, has_side_effects=True, vmem_limit_bytes=63 * 1024 * 1024
        ),
        cost_estimate=pl.CostEstimate(
            flops=2 * SIDE * rows * (width * width + span * span + queries * width * span),
            bytes_accessed=2 * (8 * width * width + span * span), transcendentals=0,
        ),
    )(activations, out_grads, in_basis, out_basis, eigenvalues, query_grads)
    return out[:, :queries]


def plain_scores(activations, out_grads, in_basis, out_basis, eigenvalues, query_grads):
    partial_out = jnp.dot(
        lax.all_gather(out_grads, "oeig", axis=0, tiled=True),
        out_basis,
        preferred_element_type=jnp.float32,
    )
    rotated_out = lax.psum(partial_out.astype(jnp.bfloat16), "ieig")
    partial_in = jnp.dot(
        lax.all_gather(activations, "ieig", axis=0, tiled=True),
        in_basis,
        preferred_element_type=jnp.float32,
    )
    rotated_in = lax.psum(partial_in.astype(jnp.bfloat16), "oeig")
    damped = (query_grads.astype(jnp.float32) / (eigenvalues.astype(jnp.float32) + DAMPING)).astype(
        jnp.bfloat16
    )
    contracted = jnp.einsum("ti,moi->mto", rotated_in, damped, preferred_element_type=jnp.float32)
    partial_score = jnp.sum(contracted * rotated_out.astype(jnp.float32)[None], axis=2).T
    row_count = partial_score.shape[0] // lax.axis_size(("oeig", "ieig"))
    first_row = lax.axis_index(("oeig", "ieig")) * row_count
    summed = lax.psum(partial_score, ("oeig", "ieig"))
    return lax.dynamic_slice_in_dim(summed, first_row, row_count, 0)


def local(
    fused, activations, out_grads, in_basis, out_basis, eigenvalues, query_grads, seq_lang,
    query_lang,
):
    scores = fused_scores if fused else plain_scores
    own_rows = scores(activations, out_grads, in_basis, out_basis, eigenvalues, query_grads)
    row_count = own_rows.shape[0]
    first_row = lax.axis_index(("oeig", "ieig")) * row_count
    seq_index = (first_row + jnp.arange(row_count, dtype=jnp.int32)) // SEQ
    onehot = seq_index[:, None] == jnp.arange(seq_lang.shape[0], dtype=jnp.int32)[None, :]
    row_lang = jnp.sum(jnp.where(onehot, seq_lang[None, :], 0), axis=1)
    matched = row_lang[:, None] == query_lang[None, :]
    factor = jnp.where(matched, 1.0, 0.5).astype(jnp.float32)
    return own_rows * (1.0 / math.sqrt(OUT * IN)) * factor


def solution(mesh):
    fused = mesh.shape["oeig"] == SIDE and mesh.shape["ieig"] == SIDE
    return jax.shard_map(
        functools.partial(local, fused),
        mesh=mesh,
        in_specs=(
            P(("groups", "ieig"), "oeig"),
            P(("groups", "oeig"), "ieig"),
            P("oeig", "ieig"),
            P("ieig", "oeig"),
            P("oeig", "ieig"),
            P(None, "oeig", "ieig"),
            P("groups"),
            P(),
        ),
        out_specs=P(("groups", "oeig", "ieig"), None),
        check_vma=False,
    )
```

```python
import functools
import math

import jax
import jax.numpy as jnp
from jax import lax
from jax.experimental import pallas as pl
from jax.experimental.pallas import tpu as pltpu
from jax.sharding import PartitionSpec as P

OUT = 16384
IN = 8192
SEQ = 32


DAMPING = 0.1
MESH = pl.DeviceIdType.MESH
F32 = jnp.float32
BF16 = jnp.bfloat16

SIDE = 4
PIECES = 2
TILE = 512
DROWS = 128
STRIP = 16


def reciprocal(x):
    guess = pl.reciprocal(x, approx=True)
    return guess * (2.0 - x * guess)


def kernel(
    act_hbm, og_hbm, ib_hbm, ob_hbm, eig_hbm, qg_hbm,
    out_ref, d_hbm,
    og, act, rip, prec, srec, ro, crecv, xrecv, frecv, w, wbuf, qbuf, ebuf, dbuf, sc, rsc,
    lsem, wsem, qsem, esem, dsem,
    ring_s, ring_r, act_s, act_r, c_s, c_r, x_s, x_r, f_s, f_r, p_s, p_r, s_s, s_r, sc_s, sc_r,
):
    a, b = lax.axis_index("oeig"), lax.axis_index("ieig")
    me = a * SIDE + b
    rows = og.shape[1]
    piece = rows // PIECES
    chunks = SIDE * PIECES
    width = og.shape[2]
    half = width // 2
    span = act.shape[2]
    queries = d_hbm.shape[0]
    core = lax.rem(b, 2)
    mate = b + 1 - 2 * core
    across = lax.rem(b + 2, SIDE)
    ring_next = lax.rem(2 * a + 1, 5)
    act_owner = [b, mate, across, lax.rem(mate + 2, SIDE)]

    def remote(src, dst, send, recv, to_a, to_b):
        return pltpu.make_async_remote_copy(
            src_ref=src, dst_ref=dst, send_sem=send, recv_sem=recv,
            device_id={"oeig": to_a, "ieig": to_b}, device_id_type=MESH,
        )

    barrier = pltpu.get_barrier_semaphore()
    others = SIDE * SIDE - 1

    @pl.loop(1, others + 1)
    def _(k):
        peer = lax.rem(me + k, SIDE * SIDE)
        pl.semaphore_signal(
            barrier, inc=1, device_id={"oeig": peer // SIDE, "ieig": lax.rem(peer, SIDE)},
            device_id_type=MESH,
        )

    own_og = pltpu.make_async_copy(og_hbm, og.at[0], lsem.at[0])
    own_act = pltpu.make_async_copy(act_hbm, act.at[0], lsem.at[1])
    own_og.start()
    own_act.start()
    pl.semaphore_wait(barrier, others)

    def ring(step):
        src = og_hbm if step == 1 else og.at[step - 1]
        return remote(src, og.at[step], ring_s.at[step], ring_r.at[step], ring_next, b)

    act_x = remote(act_hbm, act.at[2], act_s.at[2], act_r.at[2], a, across)
    act_c = remote(act_hbm, act.at[1], act_s.at[1], act_r.at[1], a, mate)
    act_f = remote(act.at[2], act.at[3], act_s.at[3], act_r.at[3], a, mate)
    act_x.start()
    act_c.start()
    ring(1).start()

    tiles = span // TILE

    def tile_copy(kind, k):
        slot = lax.rem(k, 2)
        if kind == "out":
            source, view = ob_hbm.at[:, columns(k)], wbuf.at[slot]
        elif kind == "in":
            source, view = ib_hbm.at[:, columns(k)], wbuf.at[slot, pl.ds(0, span), :]
        else:
            source, view = d_hbm.at[k // tiles, :, columns(lax.rem(k, tiles))], wbuf.at[slot]
        return pltpu.make_async_copy(source, view, wsem.at[slot])

    def stream(kind, count, compute, ahead):
        def copy(k):
            return tile_copy(kind, k)

        @pl.loop(0, count)
        def _(k):
            @pl.when(k + 1 < count)
            def _():
                copy(k + 1).start()

            if ahead is not None:

                @pl.when(k + 1 == count)
                def _():
                    tile_copy(ahead, jnp.int32(0)).start()

            copy(k).wait()
            compute(k, wbuf.at[lax.rem(k, 2)])

    def columns(k):
        return pl.ds(pl.multiple_of(k * TILE, TILE), TILE)

    def strips(count, body):
        @pl.loop(0, count // STRIP)
        def _(i):
            body(pl.ds(pl.multiple_of(i * STRIP, STRIP), STRIP))

    my_half = pl.ds(pl.multiple_of(core * half, half), half)
    other_half = pl.ds(pl.multiple_of((1 - core) * half, half), half)
    my_rows, other_rows = my_half, other_half

    def to_mate(s):
        return remote(ro.at[s, :, other_half], crecv.at[s], c_s.at[s], c_r.at[s], a, mate)

    def to_across(s):
        return remote(crecv.at[s], xrecv.at[s], x_s.at[s], x_r.at[s], a, across)

    def whole_to_mate(s):
        return remote(ro.at[s, :, my_half], frecv.at[s], f_s.at[s], f_r.at[s], a, mate)

    def rotate_out(s, ahead):
        def compute(k, tile):
            part = jnp.dot(og[s], tile[...], preferred_element_type=F32)
            ro[s, :, columns(k)] = part.astype(BF16)

        stream("out", width // TILE, compute, ahead)
        to_mate(s).start()

    def sum_cores(s):
        to_mate(s).wait_recv()

        def body(r):
            crecv[s, r, :] = (
                crecv[s, r, :].astype(F32) + ro[s, r, my_half].astype(F32)
            ).astype(BF16)

        strips(rows, body)
        to_across(s).start()

    def sum_across(s):
        to_across(s).wait_recv()

        def body(r):
            ro[s, r, my_half] = (
                crecv[s, r, :].astype(F32) + xrecv[s, r, :].astype(F32)
            ).astype(BF16)

        strips(rows, body)
        whole_to_mate(s).start()

    def rotate_in(ahead):
        def compute(k, tile):
            for s in range(SIDE):
                part = jnp.dot(
                    act[s], tile[pl.ds(0, span), :], preferred_element_type=F32
                ).astype(BF16)
                for h in range(PIECES):
                    rip[act_owner[s] * PIECES + h, :, columns(k)] = part[
                        h * piece : (h + 1) * piece
                    ]

        stream("in", span // TILE, compute, ahead)

    def damp(first, last):
        def block(k):
            return pl.ds(pl.multiple_of(k * DROWS, DROWS), DROWS)

        def loads(k):
            v = lax.rem(k, 2)
            return (
                pltpu.make_async_copy(qg_hbm.at[:, block(k), :], qbuf.at[v], qsem.at[v]),
                pltpu.make_async_copy(eig_hbm.at[block(k), :], ebuf.at[v], esem.at[v]),
            )

        def store(k):
            v = lax.rem(k, 2)
            return pltpu.make_async_copy(dbuf.at[v], d_hbm.at[:, block(k), :], dsem.at[v])

        for c in loads(jnp.int32(first)):
            c.start()

        @pl.loop(first, last)
        def _(k):
            v = lax.rem(k, 2)

            @pl.when(k + 1 < last)
            def _():
                for c in loads(k + 1):
                    c.start()

            for c in loads(k):
                c.wait()

            @pl.when(k >= first + 2)
            def _():
                store(k - 2).wait()

            def body(r):
                inv = reciprocal(ebuf[v, r, :].astype(F32) + DAMPING)
                for m in range(queries):
                    dbuf[v, m, r, :] = (qbuf[v, m, r, :].astype(F32) * inv).astype(BF16)

            strips(DROWS, body)
            store(k).start()

        for k in (last - 2, last - 1):
            store(jnp.int32(k)).wait()

    def contract(s, count, ahead):
        for k in range(s, s + count):
            whole_to_mate(k).wait_recv()
        slots = pl.ds(s, count)

        def compute(k, tile):
            mine = ro[slots, :, my_half].reshape(count * rows, half)
            theirs = frecv[slots].reshape(count * rows, half)
            got = jnp.dot(mine, tile[my_rows, :], preferred_element_type=F32)
            got = got + jnp.dot(theirs, tile[other_rows, :], preferred_element_type=F32)
            w[slots, :, columns(k)] = got.reshape(count, rows, TILE)

        stream("damped", queries * tiles, compute, ahead)

    last_a = SIDE - 1
    up = lax.rem(a + 1, SIDE)
    down = lax.rem(a + last_a, SIDE)

    def going_up(c):
        return remote(prec.at[c], prec.at[c], p_s.at[c], p_r.at[c], up, b)

    def outgoing(c):
        start = pl.multiple_of(lax.rem(c, PIECES) * piece, piece)
        return act.at[lax.div(c, PIECES), pl.ds(start, piece), :]

    def going_down(c):
        return remote(outgoing(c), srec.at[c], s_s.at[c], s_r.at[c], down, b)

    def chain(step):
        c = step - a

        @pl.when((c >= 0) & (c < chunks))
        def _():
            @pl.when(a == 0)
            def _():
                def body(r):
                    prec[c, r, :] = rip[c, r, :]

                strips(piece, body)

            @pl.when(a > 0)
            def _():
                going_up(c).wait_recv()

                def body(r):
                    prec[c, r, :] = (
                        prec[c, r, :].astype(F32) + rip[c, r, :].astype(F32)
                    ).astype(BF16)

                strips(piece, body)

            @pl.when(a < last_a)
            def _():
                going_up(c).start()

        e = step - (last_a - a)

        @pl.when((e >= 0) & (e < chunks))
        def _():
            @pl.when(a == last_a)
            def _():
                def body(r):
                    srec[e, r, :] = jnp.zeros_like(srec[e, r, :])
                    outgoing(e)[r, :] = rip[e, r, :]

                strips(piece, body)

            @pl.when(a < last_a)
            def _():
                going_down(e).wait_recv()

                def body(r):
                    outgoing(e)[r, :] = (
                        srec[e, r, :].astype(F32) + rip[e, r, :].astype(F32)
                    ).astype(BF16)

                strips(piece, body)

            @pl.when(a > 0)
            def _():
                going_down(e).start()

    lane = lax.broadcasted_iota(jnp.int32, (STRIP, sc.shape[2]), 1)
    per = sc.shape[1]
    parcels = piece // per

    def place(i):
        return i + (i // 2) * (1 - 2 * lax.rem(i, 2))

    def score(peer):
        k = lax.rem(peer - me + SIDE * SIDE, SIDE * SIDE)
        return k, remote(
            sc.at[peer], rsc.at[k], sc_s.at[k], sc_r.at[k], peer // SIDE, peer % SIDE
        )

    def finish(c):
        j, h = c // PIECES, c % PIECES
        s = lax.rem(place(a) - (j ^ (j >> 1)) + SIDE, SIDE)

        @pl.loop(0, piece // STRIP)
        def _(i):
            r = pl.ds(pl.multiple_of(i * STRIP, STRIP), STRIP)
            total = prec[c, r, :].astype(F32) + srec[c, r, :].astype(F32)
            wr = pl.ds(pl.multiple_of(h * piece + i * STRIP, STRIP), STRIP)
            packed = jnp.zeros(lane.shape, F32)
            for m in range(queries):
                got = jnp.sum(
                    total * w[s, wr, m * span : (m + 1) * span], axis=1, keepdims=True
                )
                packed = jnp.where(lane == m, got, packed)
            row = i * STRIP
            at = pl.ds(pl.multiple_of(lax.rem(row, per), STRIP), STRIP)
            sc[c * parcels + lax.div(row, per), at, :] = packed

        for peer in range(c * parcels, (c + 1) * parcels):
            k, copy = score(peer)

            @pl.when(k == 0)
            def _():
                rsc[0] = sc[peer]

            @pl.when(k > 0)
            def _():
                copy.start()

    dtiles = d_hbm.shape[1] // DROWS

    tile_copy("out", jnp.int32(0)).start()
    own_og.wait()
    rotate_out(0, "in")
    own_act.wait()
    act_x.wait_recv()
    act_f.start()
    act_c.wait_recv()
    sum_cores(0)
    act_f.wait_recv()
    rotate_in("out")
    for c in (act_x, act_c, act_f):
        c.wait_send()
    chain(0)
    damp(0, dtiles // 2)
    sum_across(0)

    ring(1).wait_recv()
    ring(2).start()
    rotate_out(1, "out")
    chain(1)
    damp(dtiles // 2, dtiles)
    sum_cores(1)
    chain(2)

    ring(2).wait_recv()
    ring(3).start()
    rotate_out(2, "damped")
    sum_across(1)
    chain(3)
    contract(0, 2, "out")
    sum_cores(2)
    chain(4)
    sum_across(2)
    chain(5)

    ring(3).wait_recv()
    rotate_out(3, "damped")
    chain(6)
    sum_cores(3)
    contract(2, 1, "damped")
    chain(7)
    sum_across(3)
    chain(8)
    contract(3, 1, None)
    done = 0
    for step in range(8, chunks + last_a):
        if step > 8:
            chain(step)
        while done <= step - last_a:
            finish(done)
            done += 1

    for step in range(1, SIDE):
        ring(step).wait_send()
    for s in range(SIDE):
        to_mate(s).wait_send()
        to_across(s).wait_send()
        whole_to_mate(s).wait_send()

    @pl.loop(0, chunks)
    def _(c):
        @pl.when(a < last_a)
        def _():
            going_up(c).wait_send()

        @pl.when(a > 0)
        def _():
            going_down(c).wait_send()

    for peer in range(SIDE * SIDE):
        k, copy = score(peer)

        @pl.when(k > 0)
        def _():
            copy.wait()

    total = rsc[0]
    for k in range(1, SIDE * SIDE):
        total = total + rsc[k]
    out_ref[...] = total


def fused_scores(activations, out_grads, in_basis, out_basis, eigenvalues, query_grads):
    rows, span = activations.shape
    width = out_grads.shape[1]
    queries = query_grads.shape[0]
    chunks, piece = SIDE * PIECES, rows // PIECES
    devices = SIDE * SIDE
    per = SIDE * rows // devices
    vmem = pltpu.VMEM
    dma = pltpu.SemaphoreType.DMA
    any_space = pl.BlockSpec(memory_space=pl.ANY)
    out, _ = pl.pallas_call(
        kernel,
        out_shape=(
            jax.ShapeDtypeStruct((per, 128), F32),
            jax.ShapeDtypeStruct(query_grads.shape, BF16),
        ),
        in_specs=[any_space] * 6,
        out_specs=(pl.BlockSpec(memory_space=pltpu.VMEM), any_space),
        scratch_shapes=[
            vmem((SIDE, rows, width), BF16),
            vmem((SIDE, rows, span), BF16),
            vmem((chunks, piece, span), BF16),
            vmem((chunks, piece, span), BF16),
            vmem((chunks, piece, span), BF16),
            vmem((SIDE, rows, width), BF16),
            vmem((SIDE, rows, width // 2), BF16),
            vmem((SIDE, rows, width // 2), BF16),
            vmem((SIDE, rows, width // 2), BF16),
            vmem((SIDE, rows, queries * span), F32),
            vmem((2, width, TILE), BF16),
            vmem((2, queries, DROWS, span), BF16),
            vmem((2, DROWS, span), BF16),
            vmem((2, queries, DROWS, span), BF16),
            vmem((devices, per, 128), F32),
            vmem((devices, per, 128), F32),
        ]
        + [dma((2,))] * 5
        + [dma((SIDE,))] * 10
        + [dma((chunks,))] * 4
        + [dma((devices,))] * 2,
        compiler_params=pltpu.CompilerParams(
            collective_id=0, has_side_effects=True, vmem_limit_bytes=63 * 1024 * 1024
        ),
        cost_estimate=pl.CostEstimate(
            flops=2 * SIDE * rows * (width * width + span * span + queries * width * span),
            bytes_accessed=2 * (8 * width * width + span * span), transcendentals=0,
        ),
    )(activations, out_grads, in_basis, out_basis, eigenvalues, query_grads)
    return out[:, :queries]


def plain_scores(activations, out_grads, in_basis, out_basis, eigenvalues, query_grads):
    partial_out = jnp.dot(
        lax.all_gather(out_grads, "oeig", axis=0, tiled=True),
        out_basis,
        preferred_element_type=jnp.float32,
    )
    rotated_out = lax.psum(partial_out.astype(jnp.bfloat16), "ieig")
    partial_in = jnp.dot(
        lax.all_gather(activations, "ieig", axis=0, tiled=True),
        in_basis,
        preferred_element_type=jnp.float32,
    )
    rotated_in = lax.psum(partial_in.astype(jnp.bfloat16), "oeig")
    damped = (query_grads.astype(jnp.float32) / (eigenvalues.astype(jnp.float32) + DAMPING)).astype(
        jnp.bfloat16
    )
    contracted = jnp.einsum("ti,moi->mto", rotated_in, damped, preferred_element_type=jnp.float32)
    partial_score = jnp.sum(contracted * rotated_out.astype(jnp.float32)[None], axis=2).T
    row_count = partial_score.shape[0] // lax.axis_size(("oeig", "ieig"))
    first_row = lax.axis_index(("oeig", "ieig")) * row_count
    summed = lax.psum(partial_score, ("oeig", "ieig"))
    return lax.dynamic_slice_in_dim(summed, first_row, row_count, 0)


def local(
    fused, activations, out_grads, in_basis, out_basis, eigenvalues, query_grads, seq_lang,
    query_lang,
):
    scores = fused_scores if fused else plain_scores
    own_rows = scores(activations, out_grads, in_basis, out_basis, eigenvalues, query_grads)
    row_count = own_rows.shape[0]
    first_row = lax.axis_index(("oeig", "ieig")) * row_count
    seq_index = (first_row + jnp.arange(row_count, dtype=jnp.int32)) // SEQ
    onehot = seq_index[:, None] == jnp.arange(seq_lang.shape[0], dtype=jnp.int32)[None, :]
    row_lang = jnp.sum(jnp.where(onehot, seq_lang[None, :], 0), axis=1)
    matched = row_lang[:, None] == query_lang[None, :]
    factor = jnp.where(matched, 1.0, 0.5).astype(jnp.float32)
    return own_rows * (1.0 / math.sqrt(OUT * IN)) * factor


def solution(mesh):
    fused = mesh.shape["oeig"] == SIDE and mesh.shape["ieig"] == SIDE
    return jax.shard_map(
        functools.partial(local, fused),
        mesh=mesh,
        in_specs=(
            P(("groups", "ieig"), "oeig"),
            P(("groups", "oeig"), "ieig"),
            P("oeig", "ieig"),
            P("ieig", "oeig"),
            P("oeig", "ieig"),
            P(None, "oeig", "ieig"),
            P("groups"),
            P(),
        ),
        out_specs=P(("groups", "oeig", "ieig"), None),
        check_vma=False,
    )
```
